32 devices in a mesh: groups: 2 (over y), dp: 8 (over z, x), tensor: 2 (over core).
Axes of the slice: x: 2, y: 2, z: 4, core: 2. Of those that a mesh axis runs over, the one named last changes fastest.
Arguments:
- tokens: bfloat16 [128, 8192], P(('groups', 'dp'), 'tensor'), parts along dimension 0, may hold values from -6 to 6
- request_adapter_index: int32 [128], P(('groups', 'dp')), parts along dimension 0, may hold values from 0 to 7
- adapter_storage_slot: int32 [16], P('groups'), parts along dimension 0, may hold values from 0 to 7, each once
- adapter_down_weight: bfloat16 [16, 32, 8192], P(('groups', 'dp'), None, 'tensor'), parts along dimension 0, may hold values from -0.0625 to 0.0625
- adapter_up_weight: bfloat16 [16, 32, 28672], P(('groups', 'dp'), None, 'tensor'), parts along dimension 0, may hold values from -1.5 to 1.5
- gate_projected_base: bfloat16 [128, 28672], P(('groups', 'dp'), 'tensor'), parts along dimension 0, may hold values from -6 to 6
- up_projected_base: bfloat16 [128, 28672], P(('groups', 'dp'), 'tensor'), parts along dimension 0, may hold values from -6 to 6
Outputs:
- hidden: bfloat16 [128, 28672], P(('groups', 'dp'), 'tensor'), parts along dimension 0
The draws below stay inside these ranges and needn't reach their ends.
There are 2 independent parts, one for each index of `groups`. The reference program is written for one: setup_inputs(seed, part) draws one part's arguments, and reference() takes and returns one part's arrays. A program takes and returns all parts, laid end to end along the dimension named above; each array names one. Nothing has to cross between parts.
Inputs may be any that keep to these rules, and one draw needn't show every extreme that they name: `adapter_storage_slot`: each slot appears exactly once.
All inputs are finite; a program needn't handle non-finite values.
Results may differ from the reference program's by a relative error of at most 0.0062.
Values may be sent and summed in bfloat16 or wider, within the bound.
A program may use at most 64 MiB of HBM per device.

```python
import math
import jax
import jax.numpy as jnp
import numpy as np
from jax import lax

MODEL_WIDTH = 8192
HIDDEN_UNITS = 28672
ADAPTER_RANK = 16
ADAPTER_TOTAL = 8
TOKENS = 64


def touch_ends(entries, own_key, low, largest):
    longest = entries.shape.index(max(entries.shape))
    spots = []
    for shift in (0, 1):
        where = [jax.random.randint(jax.random.fold_in(own_key, axis), (), 0, length) for axis, length in enumerate(entries.shape)]
        where[longest] = (where[longest] + shift) % entries.shape[longest]
        spots.append(tuple(where))
    return entries.at[spots[0]].set(low).at[spots[1]].set(largest)


def block_levels(key, dims, pieces, smallest, largest):
    loudness, own = 1.0, jax.random.fold_in(key, 6)
    for dim, shards_of in pieces:
        steps = jnp.exp(jax.random.uniform(jax.random.fold_in(own, dim), (shards_of,), jnp.float32, smallest / len(pieces), largest / len(pieces)))
        loudness = loudness * jnp.repeat(steps, dims[dim] // shards_of).reshape([-1 if axis == dim else 1 for axis in range(len(dims))])
    return loudness


def rank_bounds(count, lean):
    loads = [(1 << 20) // math.isqrt(grade ** lean) + 1 for grade in range(1, count + 1)]
    spread = 1 + sum(loads) // (1 << 30)
    return np.cumsum(np.array([max(1, weight // spread) for weight in loads]))


def ranked(rng, shape, number_of, lean):
    listing = rank_bounds(number_of, lean)
    ticket = jax.random.randint(jax.random.fold_in(rng, 1), shape, 0, int(listing[number_of - 1]))
    rank = jnp.searchsorted(jnp.asarray(listing, jnp.int32), ticket, side="right")
    return jax.random.permutation(jax.random.fold_in(rng, 2), number_of)[rank].astype(jnp.int32)


def normal_values(rng, dims, width, most, split=(), held_as=jnp.bfloat16):
    array = width * jax.random.normal(rng, dims, jnp.float32)
    if split:
        array = array * block_levels(rng, dims, split, -0.22, 0.18)
    return jnp.clip(array, -most, most).astype(held_as)


def setup_inputs(seed: int = 0, part: int = 0) -> dict:
    arg_keys = jax.random.split(jax.random.key(seed), 8)
    part_keys = jax.random.split(jax.random.fold_in(arg_keys[7], part), 8)
    return {
        "tokens": normal_values(part_keys[0], (TOKENS, MODEL_WIDTH), 1.0, 6.0, ((0, 8), (1, 2))),
        "request_adapter_index": touch_ends(ranked(part_keys[1], (TOKENS,), ADAPTER_TOTAL, 2), jax.random.fold_in(part_keys[1], 3), 0, ADAPTER_TOTAL - 1).astype(jnp.int32),
        "adapter_storage_slot": jax.random.permutation(part_keys[2], ADAPTER_TOTAL).astype(jnp.int32),
        "adapter_down_weight": normal_values(part_keys[3], (ADAPTER_TOTAL, 2 * ADAPTER_RANK, MODEL_WIDTH), MODEL_WIDTH ** -0.5, 0.0625, ((0, 8), (2, 2))),
        "adapter_up_weight": normal_values(part_keys[4], (ADAPTER_TOTAL, 2 * ADAPTER_RANK, HIDDEN_UNITS), ADAPTER_RANK ** -0.5, 1.5, ((0, 8), (2, 2))),
        "gate_projected_base": normal_values(part_keys[5], (TOKENS, HIDDEN_UNITS), 1.0, 6.0, ((0, 8), (1, 2))),
        "up_projected_base": normal_values(part_keys[6], (TOKENS, HIDDEN_UNITS), 1.0, 6.0, ((0, 8), (1, 2))),
    }


def reference(tokens, request_adapter_index, adapter_storage_slot, adapter_down_weight, adapter_up_weight, gate_projected_base, up_projected_base):
    row_slots = adapter_storage_slot[request_adapter_index].astype(jnp.int32)
    block_row_span = math.gcd(TOKENS, 16)
    block_count = TOKENS // block_row_span

    def per_block(block_args):
        input_block, storage_slot_block = block_args
        down_row_span = adapter_down_weight[storage_slot_block].astype(jnp.float32)
        low_rows = jnp.einsum("rkd,rd->rk", down_row_span, input_block.astype(jnp.float32))
        low_round = lax.optimization_barrier(low_rows.astype(jnp.bfloat16)).astype(jnp.float32)
        up_row_span = adapter_up_weight[storage_slot_block].astype(jnp.float32).reshape(block_row_span, 2, ADAPTER_RANK, HIDDEN_UNITS)
        delta_rows = jnp.einsum("rjk,rjkf->rjf", low_round.reshape(block_row_span, 2, ADAPTER_RANK), up_row_span)
        return delta_rows.astype(jnp.bfloat16)

    deltas = lax.map(per_block, (tokens.reshape(block_count, block_row_span, MODEL_WIDTH), row_slots.reshape(block_count, block_row_span)))
    deltas = deltas.reshape(TOKENS, 2, HIDDEN_UNITS)
    gate_sum = gate_projected_base.astype(jnp.float32) + deltas[:, 0].astype(jnp.float32)
    up_sum = up_projected_base.astype(jnp.float32) + deltas[:, 1].astype(jnp.float32)
    return (jax.nn.silu(gate_sum) * up_sum).astype(jnp.bfloat16)
```

```python
import functools
import math

import jax
import jax.numpy as jnp
from jax import lax
from jax.experimental import pallas as pl
from jax.experimental.pallas import tpu as pltpu
from jax.sharding import PartitionSpec as P


def plain(
    tokens,
    request_adapter_index,
    adapter_storage_slot,
    adapter_down_weight,
    adapter_up_weight,
    gate_projected_base,
    up_projected_base,
):
    holding_count, paired_rank, half_rank_width = adapter_down_weight.shape
    rank_size = paired_rank // 2
    ids_all = lax.all_gather(request_adapter_index, "dp", axis=0, tiled=True)
    total_rows = ids_all.shape[0]
    adapter_count = adapter_storage_slot.shape[0]
    id_match = ids_all[:, None] == jnp.arange(adapter_count, dtype=jnp.int32)[None, :]
    slot_all = jnp.sum(jnp.where(id_match, adapter_storage_slot[None, :], 0), axis=1)
    flattened_down = adapter_down_weight.reshape(holding_count * paired_rank, half_rank_width)
    owner_index = lax.axis_index("dp")
    shard_rows = lax.all_gather(tokens, "dp", axis=0, tiled=True)
    row_count = shard_rows.shape[0]
    projected = jnp.einsum(
        "md,cd->mc", shard_rows, flattened_down, preferred_element_type=jnp.float32
    )
    projected = projected.reshape(row_count, holding_count, paired_rank)
    local_slot = slot_all - owner_index * holding_count
    picker = (local_slot[:, None] == jnp.arange(holding_count, dtype=jnp.int32)[None, :]).astype(
        jnp.float32
    )
    term_rows = jnp.sum(projected * picker[:, :, None], axis=1)
    low_rank = lax.psum(term_rows, ("dp", "tensor"))
    low_bf = low_rank.astype(jnp.bfloat16)
    up_cols = lax.all_to_all(
        adapter_up_weight.reshape(holding_count * paired_rank, adapter_up_weight.shape[2]),
        "dp",
        split_axis=1,
        concat_axis=0,
        tiled=True,
    )
    narrow = up_cols.shape[1]
    up_four = up_cols.reshape(adapter_count, 2, rank_size, narrow)
    block_row_span = math.gcd(total_rows, 256)
    block_count = total_rows // block_row_span
    adapter_range = jnp.arange(adapter_count, dtype=jnp.int32)

    def expand(block_args):
        low_block, storage_slot_block = block_args
        onehot = (storage_slot_block[:, None] == adapter_range[None, :]).astype(jnp.bfloat16)
        spread = onehot[:, :, None, None] * low_block.reshape(block_row_span, 1, 2, rank_size)
        update = jnp.einsum("rajk,ajkf->rjf", spread, up_four, preferred_element_type=jnp.float32)
        return update.astype(jnp.bfloat16)

    deltas = lax.map(
        expand,
        (
            low_bf.reshape(block_count, block_row_span, paired_rank),
            slot_all.reshape(block_count, block_row_span),
        ),
    )
    deltas = deltas.reshape(total_rows, 2, narrow)
    home_rows = lax.all_to_all(deltas, "dp", split_axis=0, concat_axis=2, tiled=True)
    gate_sum = gate_projected_base.astype(jnp.float32) + home_rows[:, 0].astype(jnp.float32)
    up_sum = up_projected_base.astype(jnp.float32) + home_rows[:, 1].astype(jnp.float32)
    return (jax.nn.silu(gate_sum) * up_sum).astype(jnp.bfloat16)


MESH = pl.DeviceIdType.MESH
LANES = 128


def kernel(
    n,
    parts,
    ids,
    storage,
    tokens,
    down,
    up,
    gate_base,
    up_base,
    out,
    tok_send,
    tok_all,
    pair_send,
    pair_recv,
    low_all,
    up_all,
    delta_send,
    delta_recv,
    gate_vmem,
    up_vmem,
    tok_ssem,
    tok_rsem,
    pair_sem,
    low_ssem,
    low_rsem,
    up_ssem,
    up_rsem,
    delta_ssem,
    delta_rsem,
    local_sem,
):
    group = lax.axis_index("groups")
    me = lax.axis_index("dp")
    core = lax.axis_index("tensor")
    rows, width = tokens.shape
    half = width // 2
    pair_rank = down.shape[0]
    narrow = up_all.shape[2]
    total = n * rows

    def at(peer):
        return (group, peer, core)

    peers = [lax.rem(me + step, n) for step in range(1, n)]

    barrier = pltpu.get_barrier_semaphore()
    for peer in peers:
        pl.semaphore_signal(barrier, inc=1, device_id=at(peer), device_id_type=MESH)
    pl.semaphore_signal(barrier, inc=1, device_id=(group, me, 1 - core), device_id_type=MESH)

    bases = [
        pltpu.make_async_copy(gate_base, gate_vmem, local_sem.at[0]),
        pltpu.make_async_copy(up_base, up_vmem, local_sem.at[1]),
    ]
    own_columns = pl.ds(pl.multiple_of(me * narrow, LANES), narrow)
    own_up = pltpu.make_async_copy(up.at[:, own_columns], up_all.at[me], local_sem.at[2])
    own_up.start()
    for copy in bases:
        copy.start()

    slot_rows = lax.broadcasted_iota(jnp.int32, (rows, LANES), 0)
    slots = jnp.zeros((rows, LANES), jnp.int32)
    for row in range(rows):
        slots = jnp.where(slot_rows == row, storage[ids[row]], slots)
    slots = slots.astype(jnp.float32)
    values = tokens[...].astype(jnp.float32)
    packed = jnp.concatenate(
        [
            jnp.concatenate([values[:, :half], slots], axis=1),
            jnp.concatenate([values[:, half:], slots], axis=1),
        ],
        axis=0,
    ).astype(jnp.bfloat16)
    tok_send[...] = packed
    tok_all[me] = packed

    pl.semaphore_wait(barrier, n)

    def tok_copy(peer, slot_at, sem_at):
        return pltpu.make_async_remote_copy(
            src_ref=tok_send,
            dst_ref=tok_all.at[slot_at],
            send_sem=tok_ssem.at[peer],
            recv_sem=tok_rsem.at[sem_at],
            device_id=at(peer),
            device_id_type=MESH,
        )

    def up_copy(peer, slot_at, part):
        start, size = parts[part]
        columns = pl.ds(pl.multiple_of(peer * narrow + start, LANES), size)
        return pltpu.make_async_remote_copy(
            src_ref=up.at[:, columns],
            dst_ref=up_all.at[slot_at, :, pl.ds(start, size)],
            send_sem=up_ssem.at[peer, part],
            recv_sem=up_rsem.at[slot_at, part],
            device_id=at(peer),
            device_id_type=MESH,
        )

    def low_copy(peer, slot_at):
        return pltpu.make_async_remote_copy(
            src_ref=low_all.at[me],
            dst_ref=low_all.at[slot_at],
            send_sem=low_ssem.at[peer],
            recv_sem=low_rsem.at[slot_at],
            device_id=at(peer),
            device_id_type=MESH,
        )

    def delta_copy(peer, slot_at, part):
        start, size = parts[part]
        columns = pl.ds(start, size)
        return pltpu.make_async_remote_copy(
            src_ref=delta_send.at[peer, :, columns],
            dst_ref=delta_recv.at[slot_at, :, columns],
            send_sem=delta_ssem.at[peer, part],
            recv_sem=delta_rsem.at[slot_at, part],
            device_id=at(peer),
            device_id_type=MESH,
        )

    for peer in peers:
        tok_copy(peer, me, me).start()
    for part in range(len(parts)):
        for peer in peers:
            up_copy(peer, me, part).start()

    repeat = LANES // pair_rank
    first, second = down[:, :half], down[:, half:]
    weights = jnp.concatenate([first] * repeat + [second] * repeat, axis=0)
    for peer in peers:
        tok_copy(peer, peer, peer).wait_recv()
    arrived = tok_all[...]
    product = lax.dot_general(
        arrived[:, :, :half].reshape(total * 2, half),
        weights,
        (((1,), (1,)), ((), ())),
        preferred_element_type=jnp.float32,
    ).reshape(n, 2, rows, 2 * LANES)
    slot_of = arrived[:, :, half:].astype(jnp.float32).reshape(n, 2, rows, LANES)[:, 0]
    lane_group = lax.broadcasted_iota(jnp.int32, (n, rows, LANES), 2) // pair_rank
    mine = (slot_of == me.astype(jnp.float32)) & (lane_group == lax.rem(me, repeat))
    low = product[:, 0, :, :LANES] + product[:, 1, :, LANES:]
    low = jnp.where(mine, low, 0.0).reshape(total, LANES)
    pair_send[...] = low
    pair = pltpu.make_async_remote_copy(
        src_ref=pair_send,
        dst_ref=pair_recv,
        send_sem=pair_sem.at[0],
        recv_sem=pair_sem.at[1],
        device_id=(group, me, 1 - core),
        device_id_type=MESH,
    )
    pair.start()
    pair.wait_recv()
    low_all[me] = (low + pair_recv[...]).astype(jnp.bfloat16)
    for peer in peers:
        low_copy(peer, me).start()
    for peer in peers:
        low_copy(peer, peer).wait_recv()

    codes = low_all[...].astype(jnp.float32)
    groups = [
        sum(codes[start + k] for k in range(repeat)) for start in range(0, n, repeat)
    ]
    spread = jnp.concatenate(groups, axis=1).reshape(n, rows, n * pair_rank)
    lane = lax.broadcasted_iota(jnp.int32, spread.shape, 2)
    is_gate = lax.rem(lane, pair_rank) < pair_rank // 2
    spread = jnp.stack(
        [jnp.where(is_gate, spread, 0.0), jnp.where(is_gate, 0.0, spread)], axis=1
    )
    spread = spread.reshape(2 * total, n * pair_rank).astype(jnp.bfloat16)

    own_up.wait()
    for part, (start, size) in enumerate(parts):
        for peer in peers:
            up_copy(peer, peer, part).wait_recv()
        columns = pl.ds(start, size)
        delta = jnp.dot(
            spread,
            up_all[:, :, columns].reshape(n * pair_rank, size),
            preferred_element_type=jnp.float32,
        )
        delta_send[:, :, columns] = delta.astype(jnp.bfloat16).reshape(n, 2 * rows, size)
        for peer in peers:
            delta_copy(peer, me, part).start()

    for copy in bases:
        copy.wait()

    def finish(source, part, block):
        start, size = parts[part]
        columns = pl.ds(pl.multiple_of(source * narrow + start, LANES), size)
        block = block.astype(jnp.float32)
        gate = gate_vmem[:, columns].astype(jnp.float32) + block[:rows]
        raised = up_vmem[:, columns].astype(jnp.float32) + block[rows:]
        out[:, columns] = (jax.nn.silu(gate) * raised).astype(out.dtype)

    for part, (start, size) in enumerate(parts):
        finish(me, part, delta_send[me, :, pl.ds(start, size)])
        for peer in peers:
            delta_copy(peer, peer, part).wait_recv()
            finish(peer, part, delta_recv[peer, :, pl.ds(start, size)])

    pair.wait_send()
    for peer in peers:
        tok_copy(peer, me, me).wait_send()
        low_copy(peer, me).wait_send()
        for part in range(len(parts)):
            up_copy(peer, me, part).wait_send()
            delta_copy(peer, me, part).wait_send()


def cut(narrow, pieces):
    tiles = narrow // LANES
    edges = [tiles * k // pieces * LANES for k in range(pieces + 1)]
    return tuple((a, b - a) for a, b in zip(edges, edges[1:]) if b > a)


def local(mesh, *arrays):
    tokens, ids, storage, down, up, gate_base, up_base = arrays
    n = mesh.shape["dp"]
    rows, width = tokens.shape
    held, pair_rank, _ = down.shape
    hidden = up.shape[2]
    fits = (
        held == 1
        and mesh.shape["tensor"] == 2
        and hidden % (n * LANES) == 0
        and rows == 8
        and width % (2 * LANES) == 0
        and pair_rank % 16 == 0
        and LANES % pair_rank == 0
        and (n * pair_rank) % LANES == 0
        and n <= 8
    )
    if not fits:
        return plain(*arrays)
    narrow = hidden // n
    parts = cut(narrow, 2)
    count = len(parts)
    vmem = pl.BlockSpec(memory_space=pltpu.VMEM)
    smem = pl.BlockSpec(memory_space=pltpu.SMEM)
    hbm = pl.BlockSpec(memory_space=pl.ANY)
    dma = pltpu.SemaphoreType.DMA
    bf16 = jnp.bfloat16
    return pl.pallas_call(
        functools.partial(kernel, n, parts),
        out_shape=jax.ShapeDtypeStruct((rows, hidden), bf16),
        in_specs=[smem, smem, vmem, vmem, hbm, hbm, hbm],
        out_specs=vmem,
        scratch_shapes=[
            pltpu.VMEM((2 * rows, width // 2 + LANES), bf16),
            pltpu.VMEM((n, 2 * rows, width // 2 + LANES), bf16),
            pltpu.VMEM((n * rows, LANES), jnp.float32),
            pltpu.VMEM((n * rows, LANES), jnp.float32),
            pltpu.VMEM((n, n * rows, LANES), bf16),
            pltpu.VMEM((n, pair_rank, narrow), bf16),
            pltpu.VMEM((n, 2 * rows, narrow), bf16),
            pltpu.VMEM((n, 2 * rows, narrow), bf16),
            pltpu.VMEM((rows, hidden), bf16),
            pltpu.VMEM((rows, hidden), bf16),
            dma((n,)),
            dma((n,)),
            dma((2,)),
            dma((n,)),
            dma((n,)),
            dma((n, count)),
            dma((n, count)),
            dma((n, count)),
            dma((n, count)),
            dma((3,)),
        ],
        compiler_params=pltpu.CompilerParams(
            collective_id=0, has_side_effects=True, vmem_limit_bytes=32 * 1024 * 1024
        ),
    )(ids, storage, tokens, down[0], up[0], gate_base, up_base)


def solution(mesh):
    in_specs = (
        P(("groups", "dp"), "tensor"),
        P(("groups", "dp")),
        P("groups"),
        P(("groups", "dp"), None, "tensor"),
        P(("groups", "dp"), None, "tensor"),
        P(("groups", "dp"), "tensor"),
        P(("groups", "dp"), "tensor"),
    )
    out_specs = P(("groups", "dp"), "tensor")
    return jax.shard_map(functools.partial(local, mesh), mesh=mesh, in_specs=in_specs, out_specs=out_specs, check_vma=False)
```

```python
import functools
import math

import jax
import jax.numpy as jnp
from jax import lax
from jax.experimental import pallas as pl
from jax.experimental.pallas import tpu as pltpu
from jax.sharding import PartitionSpec as P


def plain(
    tokens,
    request_adapter_index,
    adapter_storage_slot,
    adapter_down_weight,
    adapter_up_weight,
    gate_projected_base,
    up_projected_base,
):
    holding_count, paired_rank, half_rank_width = adapter_down_weight.shape
    rank_size = paired_rank // 2
    ids_all = lax.all_gather(request_adapter_index, "dp", axis=0, tiled=True)
    total_rows = ids_all.shape[0]
    adapter_count = adapter_storage_slot.shape[0]
    id_match = ids_all[:, None] == jnp.arange(adapter_count, dtype=jnp.int32)[None, :]
    slot_all = jnp.sum(jnp.where(id_match, adapter_storage_slot[None, :], 0), axis=1)
    flattened_down = adapter_down_weight.reshape(holding_count * paired_rank, half_rank_width)
    owner_index = lax.axis_index("dp")
    shard_rows = lax.all_gather(tokens, "dp", axis=0, tiled=True)
    row_count = shard_rows.shape[0]
    projected = jnp.einsum(
        "md,cd->mc", shard_rows, flattened_down, preferred_element_type=jnp.float32
    )
    projected = projected.reshape(row_count, holding_count, paired_rank)
    local_slot = slot_all - owner_index * holding_count
    picker = (local_slot[:, None] == jnp.arange(holding_count, dtype=jnp.int32)[None, :]).astype(
        jnp.float32
    )
    term_rows = jnp.sum(projected * picker[:, :, None], axis=1)
    low_rank = lax.psum(term_rows, ("dp", "tensor"))
    low_bf = low_rank.astype(jnp.bfloat16)
    up_cols = lax.all_to_all(
        adapter_up_weight.reshape(holding_count * paired_rank, adapter_up_weight.shape[2]),
        "dp",
        split_axis=1,
        concat_axis=0,
        tiled=True,
    )
    narrow = up_cols.shape[1]
    up_four = up_cols.reshape(adapter_count, 2, rank_size, narrow)
    block_row_span = math.gcd(total_rows, 256)
    block_count = total_rows // block_row_span
    adapter_range = jnp.arange(adapter_count, dtype=jnp.int32)

    def expand(block_args):
        low_block, storage_slot_block = block_args
        onehot = (storage_slot_block[:, None] == adapter_range[None, :]).astype(jnp.bfloat16)
        spread = onehot[:, :, None, None] * low_block.reshape(block_row_span, 1, 2, rank_size)
        update = jnp.einsum("rajk,ajkf->rjf", spread, up_four, preferred_element_type=jnp.float32)
        return update.astype(jnp.bfloat16)

    deltas = lax.map(
        expand,
        (
            low_bf.reshape(block_count, block_row_span, paired_rank),
            slot_all.reshape(block_count, block_row_span),
        ),
    )
    deltas = deltas.reshape(total_rows, 2, narrow)
    home_rows = lax.all_to_all(deltas, "dp", split_axis=0, concat_axis=2, tiled=True)
    gate_sum = gate_projected_base.astype(jnp.float32) + home_rows[:, 0].astype(jnp.float32)
    up_sum = up_projected_base.astype(jnp.float32) + home_rows[:, 1].astype(jnp.float32)
    return (jax.nn.silu(gate_sum) * up_sum).astype(jnp.bfloat16)


MESH = pl.DeviceIdType.MESH
LANES = 128


def kernel(
    n,
    parts,
    ids,
    storage,
    tokens,
    down,
    up,
    gate_base,
    up_base,
    out,
    tok_vmem,
    tok_send,
    tok_all,
    down_all,
    sum_send,
    sum_recv,
    codes,
    wide_up,
    near_up,
    wide_send,
    near_send,
    wide_recv,
    near_recv,
    gate_vmem,
    up_vmem,
    tok_ssem,
    tok_rsem,
    down_ssem,
    down_rsem,
    sum_ssem,
    sum_rsem,
    code_ssem,
    code_rsem,
    wide_ssem,
    wide_rsem,
    near_ssem,
    near_rsem,
    back_ssem,
    back_rsem,
    local_sem,
):
    group = lax.axis_index("groups")
    me = lax.axis_index("dp")
    core = lax.axis_index("tensor")
    m = n // 2
    side, place = me // m, lax.rem(me, m)
    seat = place * 2 + core
    rows, width = tok_vmem.shape
    piece = width // m
    bit = piece // 2
    pair_rank = down.shape[0]
    wide, near = wide_up.shape[2], near_up.shape[2]
    wide_total = n * wide
    total = n * rows

    def remote(src, dst, send, recv, peer, peer_core=core):
        return pltpu.make_async_remote_copy(
            src_ref=src,
            dst_ref=dst,
            send_sem=send,
            recv_sem=recv,
            device_id=(group, peer, peer_core),
            device_id_type=MESH,
        )

    across = [(1 - side) * m + lax.rem(place + step, m) for step in range(m)]
    beside = [side * m + lax.rem(place + step, m) for step in range(1, m)]
    peers = across + beside
    seats = [lax.rem(seat + step, n) for step in range(1, n)]

    tok_load = pltpu.make_async_copy(tokens, tok_vmem, local_sem.at[0])
    tok_load.start()
    barrier = pltpu.get_barrier_semaphore()
    for peer in peers:
        for peer_core in range(2):
            pl.semaphore_signal(
                barrier, inc=1, device_id=(group, peer, peer_core), device_id_type=MESH
            )
    pl.semaphore_signal(barrier, inc=1, device_id=(group, me, 1 - core), device_id_type=MESH)

    def span(start, size):
        return pl.ds(pl.multiple_of(start, LANES), size)

    loads = [
        pltpu.make_async_copy(down.at[:, span(place * piece, piece)], down_all.at[place], local_sem.at[1]),
        pltpu.make_async_copy(up.at[:, span(me * wide, wide)], wide_up.at[me], local_sem.at[2]),
        pltpu.make_async_copy(
            up.at[:, span(wide_total + place * near, near)], near_up.at[place], local_sem.at[3]
        ),
        pltpu.make_async_copy(gate_base, gate_vmem, local_sem.at[4]),
        pltpu.make_async_copy(up_base, up_vmem, local_sem.at[5]),
    ]
    for copy in loads:
        copy.start()

    slot_rows = lax.broadcasted_iota(jnp.int32, (rows, LANES), 0)
    slots = jnp.zeros((rows, LANES), jnp.int32)
    for row in range(rows):
        slots = jnp.where(slot_rows == row, storage[ids[row]], slots)
    slots = slots.astype(jnp.float32)
    tok_load.wait()
    values = tok_vmem[...].astype(jnp.float32)
    for part in range(m):
        cut_at = part * piece
        tok_send[part] = jnp.concatenate(
            [
                jnp.concatenate([values[:, cut_at : cut_at + bit], slots], axis=1),
                jnp.concatenate([values[:, cut_at + bit : cut_at + piece], slots], axis=1),
            ],
            axis=0,
        ).astype(jnp.bfloat16)
    tok_all[me] = tok_send[place]

    pl.semaphore_wait(barrier, 2 * n - 1)

    def tok_copy(peer, index):
        return remote(
            tok_send.at[lax.rem(peer, m)], tok_all.at[index], tok_ssem.at[peer], tok_rsem.at[index], peer
        )

    def down_copy(peer, index):
        spot = lax.rem(peer, m)
        return remote(
            down.at[:, span(spot * piece, piece)],
            down_all.at[index],
            down_ssem.at[spot],
            down_rsem.at[index],
            peer,
        )

    def wide_copy(peer, index):
        return remote(
            up.at[:, span(peer * wide, wide)],
            wide_up.at[index],
            wide_ssem.at[peer],
            wide_rsem.at[index],
            peer,
        )

    def near_copy(peer, index):
        spot = lax.rem(peer, m)
        return remote(
            up.at[:, span(wide_total + spot * near, near)],
            near_up.at[index],
            near_ssem.at[spot],
            near_rsem.at[index],
            peer,
        )

    def sum_copy(other, index):
        return remote(
            sum_send.at[other],
            sum_recv.at[index],
            sum_ssem.at[other],
            sum_rsem.at[index],
            side * m + other // 2,
            lax.rem(other, 2),
        )

    def code_copy(peer, peer_core, code_side, code_seat):
        return remote(
            codes.at[side, seat],
            codes.at[code_side, code_seat],
            code_ssem.at[peer, peer_core],
            code_rsem.at[code_side, code_seat],
            peer,
            peer_core,
        )

    def back_copy(peer, index, which):
        kind, start, size = parts[which]
        send, recv = (near_send, near_recv) if kind else (wide_send, wide_recv)
        columns = pl.ds(start, size)
        return remote(
            send.at[peer, :, columns],
            recv.at[index, :, columns],
            back_ssem.at[peer, which],
            back_rsem.at[index, which],
            peer,
        )

    for peer in peers:
        tok_copy(peer, me).start()
    for peer in beside:
        down_copy(peer, place).start()
    for peer in across:
        wide_copy(peer, me).start()
    for peer in beside:
        near_copy(peer, place).start()
    for peer in beside:
        wide_copy(peer, me).start()

    loads[0].wait()
    for peer in beside:
        down_copy(peer, lax.rem(peer, m)).wait_recv()
    for peer in peers:
        tok_copy(peer, peer).wait_recv()
    arrived = tok_all[...]
    held = down_all[...].reshape(m * pair_rank, piece)
    product = lax.dot_general(
        arrived[:, :, :bit].reshape(total * 2, bit),
        jnp.concatenate([held[:, :bit], held[:, bit:]], axis=0),
        (((1,), (1,)), ((), ())),
        preferred_element_type=jnp.float32,
    ).reshape(n, 2, rows, 2 * LANES)
    slot_of = arrived[:, :, bit:].astype(jnp.float32).reshape(n, 2, rows, LANES)[:, 0]
    adapter = lax.broadcasted_iota(jnp.int32, (n, rows, LANES), 2) // pair_rank + side * m
    low = product[:, 0, :, :LANES] + product[:, 1, :, LANES:]
    low = jnp.where(slot_of == adapter.astype(jnp.float32), low, 0.0)
    sum_send[...] = low
    sum_recv[seat] = sum_send[seat]
    for other in seats:
        sum_copy(other, seat).start()
    for other in seats:
        sum_copy(other, other).wait_recv()
    codes[side, seat] = jnp.sum(sum_recv[...], axis=0)
    everyone = [(peer, peer_core) for peer in across for peer_core in (core, 1 - core)]
    everyone += [(peer, peer_core) for peer in beside for peer_core in (core, 1 - core)]
    everyone += [(me, 1 - core)]
    for peer, peer_core in everyone:
        code_copy(peer, peer_core, side, seat).start()

    def stacked(values):
        lane = lax.broadcasted_iota(jnp.int32, values.shape, 2)
        is_gate = lax.rem(lane, pair_rank) < pair_rank // 2
        both = [jnp.where(is_gate, values, 0.0), jnp.where(is_gate, 0.0, values)]
        return jnp.stack(both, axis=1).reshape(2 * total, values.shape[2]).astype(jnp.bfloat16)

    for other in seats:
        code_copy(side * m + other // 2, lax.rem(other, 2), side, other).wait_recv()
    near_codes = stacked(codes[side])
    loads[2].wait()
    for peer in beside:
        near_copy(peer, lax.rem(peer, m)).wait_recv()

    def expand(which, spread):
        kind, start, size = parts[which]
        source, send = (near_up, near_send) if kind else (wide_up, wide_send)
        columns = pl.ds(start, size)
        depth = spread.shape[1]
        delta = jnp.dot(
            spread,
            source[:, :, columns].reshape(depth, size),
            preferred_element_type=jnp.float32,
        )
        send[:, :, columns] = delta.astype(jnp.bfloat16).reshape(n, 2 * rows, size)
        for peer in peers:
            back_copy(peer, me, which).start()

    for which, (kind, _, _) in enumerate(parts):
        if kind:
            expand(which, near_codes)

    for other in range(n):
        code_copy((1 - side) * m + other // 2, other % 2, 1 - side, other).wait_recv()
    wide_codes = stacked(jnp.concatenate([codes[0], codes[1]], axis=2))
    loads[1].wait()
    for peer in peers:
        wide_copy(peer, peer).wait_recv()
    for which, (kind, _, _) in enumerate(parts):
        if not kind:
            expand(which, wide_codes)

    loads[3].wait()
    loads[4].wait()

    def finish(start, size, block):
        columns = span(start, size)
        gate = gate_vmem[:, columns].astype(jnp.float32) + block[:rows]
        raised = up_vmem[:, columns].astype(jnp.float32) + block[rows:]
        out[:, columns] = (jax.nn.silu(gate) * raised).astype(out.dtype)

    for which, (kind, start, size) in enumerate(parts):
        columns = pl.ds(start, size)
        if kind:
            for step in range(m):
                spot = lax.rem(place + step, m)
                if step:
                    mine = side * m + spot
                    back_copy(mine, mine, which).wait_recv()
                    own = near_recv[mine, :, columns]
                else:
                    own = near_send[me, :, columns]
                far = (1 - side) * m + spot
                back_copy(far, far, which).wait_recv()
                block = own.astype(jnp.float32) + near_recv[far, :, columns].astype(jnp.float32)
                finish(wide_total + spot * near + start, size, block)
        else:
            own = wide_send[me, :, columns].astype(jnp.float32)
            finish(me * wide + start, size, own)
            for peer in beside + across:
                back_copy(peer, peer, which).wait_recv()
                block = wide_recv[peer, :, columns].astype(jnp.float32)
                finish(peer * wide + start, size, block)

    for peer in peers:
        tok_copy(peer, me).wait_send()
        wide_copy(peer, me).wait_send()
        for which in range(len(parts)):
            back_copy(peer, me, which).wait_send()
    for peer in beside:
        down_copy(peer, place).wait_send()
        near_copy(peer, place).wait_send()
    for other in seats:
        sum_copy(other, seat).wait_send()
    for peer, peer_core in everyone:
        code_copy(peer, peer_core, side, seat).wait_send()


def cut(size, pieces):
    tiles = size // LANES
    edges = [tiles * k // pieces * LANES for k in range(pieces + 1)]
    return [(a, b - a) for a, b in zip(edges, edges[1:]) if b > a]


WIDE_TILES = 6
NEAR_PIECES = 2
WIDE_PIECES = 1


def local(mesh, *arrays):
    tokens, ids, storage, down, up, gate_base, up_base = arrays
    n = mesh.shape["dp"]
    rows, width = tokens.shape
    held, pair_rank, _ = down.shape
    hidden = up.shape[2]
    m = n // 2
    wide = WIDE_TILES * LANES
    near = (hidden - n * wide) // m
    fits = (
        held == 1
        and n % 2 == 0
        and n == rows == 8
        and mesh.shape["tensor"] == 2
        and m * pair_rank == LANES
        and width % (2 * m * LANES) == 0
        and near > 0
        and near % LANES == 0
        and n * wide + m * near == hidden
    )
    if not fits:
        return plain(*arrays)
    parts = [(1, *edge) for edge in cut(near, NEAR_PIECES)]
    parts += [(0, *edge) for edge in cut(wide, WIDE_PIECES)]
    count = len(parts)
    vmem = pl.BlockSpec(memory_space=pltpu.VMEM)
    smem = pl.BlockSpec(memory_space=pltpu.SMEM)
    hbm = pl.BlockSpec(memory_space=pl.ANY)
    dma = pltpu.SemaphoreType.DMA
    bf16 = jnp.bfloat16
    packed = width // (2 * m) + LANES
    return pl.pallas_call(
        functools.partial(kernel, n, parts),
        out_shape=jax.ShapeDtypeStruct((rows, hidden), bf16),
        in_specs=[smem, smem, hbm, hbm, hbm, hbm, hbm],
        out_specs=vmem,
        scratch_shapes=[
            pltpu.VMEM((rows, width), bf16),
            pltpu.VMEM((m, 2 * rows, packed), bf16),
            pltpu.VMEM((n, 2 * rows, packed), bf16),
            pltpu.VMEM((m, pair_rank, width // m), bf16),
            pltpu.VMEM((n, rows, LANES), jnp.float32),
            pltpu.VMEM((n, rows, LANES), jnp.float32),
            pltpu.VMEM((2, n, rows, LANES), jnp.float32),
            pltpu.VMEM((n, pair_rank, wide), bf16),
            pltpu.VMEM((m, pair_rank, near), bf16),
            pltpu.VMEM((n, 2 * rows, wide), bf16),
            pltpu.VMEM((n, 2 * rows, near), bf16),
            pltpu.VMEM((n, 2 * rows, wide), bf16),
            pltpu.VMEM((n, 2 * rows, near), bf16),
            pltpu.VMEM((rows, hidden), bf16),
            pltpu.VMEM((rows, hidden), bf16),
            dma((n,)),
            dma((n,)),
            dma((m,)),
            dma((m,)),
            dma((n,)),
            dma((n,)),
            dma((n, 2)),
            dma((2, n)),
            dma((n,)),
            dma((n,)),
            dma((m,)),
            dma((m,)),
            dma((n, count)),
            dma((n, count)),
            dma((6,)),
        ],
        compiler_params=pltpu.CompilerParams(
            collective_id=0, has_side_effects=True, vmem_limit_bytes=60 * 1024 * 1024
        ),
    )(ids, storage, tokens, down[0], up[0], gate_base, up_base)


def solution(mesh):
    in_specs = (
        P(("groups", "dp"), "tensor"),
        P(("groups", "dp")),
        P("groups"),
        P(("groups", "dp"), None, "tensor"),
        P(("groups", "dp"), None, "tensor"),
        P(("groups", "dp"), "tensor"),
        P(("groups", "dp"), "tensor"),
    )
    out_specs = P(("groups", "dp"), "tensor")
    return jax.shard_map(functools.partial(local, mesh), mesh=mesh, in_specs=in_specs, out_specs=out_specs, check_vma=False)
```

```python
import functools
import math

import jax
import jax.numpy as jnp
from jax import lax
from jax.experimental import pallas as pl
from jax.experimental.pallas import tpu as pltpu
from jax.sharding import PartitionSpec as P


def plain(
    tokens,
    request_adapter_index,
    adapter_storage_slot,
    adapter_down_weight,
    adapter_up_weight,
    gate_projected_base,
    up_projected_base,
):
    holding_count, paired_rank, half_rank_width = adapter_down_weight.shape
    rank_size = paired_rank // 2
    ids_all = lax.all_gather(request_adapter_index, "dp", axis=0, tiled=True)
    total_rows = ids_all.shape[0]
    adapter_count = adapter_storage_slot.shape[0]
    id_match = ids_all[:, None] == jnp.arange(adapter_count, dtype=jnp.int32)[None, :]
    slot_all = jnp.sum(jnp.where(id_match, adapter_storage_slot[None, :], 0), axis=1)
    flattened_down = adapter_down_weight.reshape(holding_count * paired_rank, half_rank_width)
    owner_index = lax.axis_index("dp")
    shard_rows = lax.all_gather(tokens, "dp", axis=0, tiled=True)
    row_count = shard_rows.shape[0]
    projected = jnp.einsum(
        "md,cd->mc", shard_rows, flattened_down, preferred_element_type=jnp.float32
    )
    projected = projected.reshape(row_count, holding_count, paired_rank)
    local_slot = slot_all - owner_index * holding_count
    picker = (local_slot[:, None] == jnp.arange(holding_count, dtype=jnp.int32)[None, :]).astype(
        jnp.float32
    )
    term_rows = jnp.sum(projected * picker[:, :, None], axis=1)
    low_rank = lax.psum(term_rows, ("dp", "tensor"))
    low_bf = low_rank.astype(jnp.bfloat16)
    up_cols = lax.all_to_all(
        adapter_up_weight.reshape(holding_count * paired_rank, adapter_up_weight.shape[2]),
        "dp",
        split_axis=1,
        concat_axis=0,
        tiled=True,
    )
    narrow = up_cols.shape[1]
    up_four = up_cols.reshape(adapter_count, 2, rank_size, narrow)
    block_row_span = math.gcd(total_rows, 256)
    block_count = total_rows // block_row_span
    adapter_range = jnp.arange(adapter_count, dtype=jnp.int32)

    def expand(block_args):
        low_block, storage_slot_block = block_args
        onehot = (storage_slot_block[:, None] == adapter_range[None, :]).astype(jnp.bfloat16)
        spread = onehot[:, :, None, None] * low_block.reshape(block_row_span, 1, 2, rank_size)
        update = jnp.einsum("rajk,ajkf->rjf", spread, up_four, preferred_element_type=jnp.float32)
        return update.astype(jnp.bfloat16)

    deltas = lax.map(
        expand,
        (
            low_bf.reshape(block_count, block_row_span, paired_rank),
            slot_all.reshape(block_count, block_row_span),
        ),
    )
    deltas = deltas.reshape(total_rows, 2, narrow)
    home_rows = lax.all_to_all(deltas, "dp", split_axis=0, concat_axis=2, tiled=True)
    gate_sum = gate_projected_base.astype(jnp.float32) + home_rows[:, 0].astype(jnp.float32)
    up_sum = up_projected_base.astype(jnp.float32) + home_rows[:, 1].astype(jnp.float32)
    return (jax.nn.silu(gate_sum) * up_sum).astype(jnp.bfloat16)


MESH = pl.DeviceIdType.MESH
LANES = 128


def kernel(
    n,
    parts,
    ids_hbm,
    storage_hbm,
    tokens,
    down,
    up,
    gate_base,
    up_base,
    out,
    ids,
    storage,
    tok_vmem,
    tok_send,
    tok_all,
    down_all,
    sum_send,
    sum_recv,
    codes,
    wide_up,
    near_up,
    wide_send,
    near_send,
    wide_recv,
    near_recv,
    gate_vmem,
    up_vmem,
    tok_ssem,
    tok_rsem,
    down_ssem,
    down_rsem,
    sum_ssem,
    sum_rsem,
    code_ssem,
    code_rsem,
    wide_ssem,
    wide_rsem,
    near_ssem,
    near_rsem,
    back_ssem,
    back_rsem,
    local_sem,
):
    group = lax.axis_index("groups")
    me = lax.axis_index("dp")
    core = lax.axis_index("tensor")
    m = n // 2
    side, place = me // m, lax.rem(me, m)
    seat = place * 2 + core
    rows, width = tok_vmem.shape
    piece = width // m
    bit = piece // 2
    pair_rank = down.shape[0]
    wide, near = wide_up.shape[2], near_up.shape[2]
    wide_total = n * wide
    total = n * rows

    def remote(src, dst, send, recv, peer, peer_core=core):
        return pltpu.make_async_remote_copy(
            src_ref=src,
            dst_ref=dst,
            send_sem=send,
            recv_sem=recv,
            device_id=(group, peer, peer_core),
            device_id_type=MESH,
        )

    across = [(1 - side) * m + lax.rem(place + step, m) for step in range(m)]
    beside = [side * m + lax.rem(place + step, m) for step in range(1, m)]
    peers = across + beside
    seats = [lax.rem(seat + step, n) for step in range(1, n)]

    tok_load = pltpu.make_async_copy(tokens, tok_vmem, local_sem.at[0])
    tok_load.start()
    index_loads = [
        pltpu.make_async_copy(ids_hbm, ids, local_sem.at[6]),
        pltpu.make_async_copy(storage_hbm, storage, local_sem.at[7]),
    ]
    for copy in index_loads:
        copy.start()
    barrier = pltpu.get_barrier_semaphore()
    for peer in peers:
        for peer_core in range(2):
            pl.semaphore_signal(
                barrier, inc=1, device_id=(group, peer, peer_core), device_id_type=MESH
            )
    pl.semaphore_signal(barrier, inc=1, device_id=(group, me, 1 - core), device_id_type=MESH)

    def span(start, size):
        return pl.ds(pl.multiple_of(start, LANES), size)

    loads = [
        pltpu.make_async_copy(down.at[:, span(place * piece, piece)], down_all.at[place], local_sem.at[1]),
        pltpu.make_async_copy(up.at[:, span(me * wide, wide)], wide_up.at[me], local_sem.at[2]),
        pltpu.make_async_copy(
            up.at[:, span(wide_total + place * near, near)], near_up.at[place], local_sem.at[3]
        ),
        pltpu.make_async_copy(gate_base, gate_vmem, local_sem.at[4]),
        pltpu.make_async_copy(up_base, up_vmem, local_sem.at[5]),
    ]
    for copy in loads:
        copy.start()

    for copy in index_loads:
        copy.wait()
    slot_rows = lax.broadcasted_iota(jnp.int32, (rows, LANES), 0)
    slots = jnp.zeros((rows, LANES), jnp.int32)
    for row in range(rows):
        slots = jnp.where(slot_rows == row, storage[ids[row]], slots)
    slots = slots.astype(jnp.float32)
    tok_load.wait()
    values = tok_vmem[...].astype(jnp.float32)
    for part in range(m):
        cut_at = part * piece
        tok_send[part] = jnp.concatenate(
            [
                jnp.concatenate([values[:, cut_at : cut_at + bit], slots], axis=1),
                jnp.concatenate([values[:, cut_at + bit : cut_at + piece], slots], axis=1),
            ],
            axis=0,
        ).astype(jnp.bfloat16)
    tok_all[me] = tok_send[place]

    pl.semaphore_wait(barrier, 2 * n - 1)

    def tok_copy(peer, index):
        return remote(
            tok_send.at[lax.rem(peer, m)], tok_all.at[index], tok_ssem.at[peer], tok_rsem.at[index], peer
        )

    def down_copy(peer, index):
        spot = lax.rem(peer, m)
        return remote(
            down.at[:, span(spot * piece, piece)],
            down_all.at[index],
            down_ssem.at[spot],
            down_rsem.at[index],
            peer,
        )

    def wide_copy(peer, index):
        return remote(
            up.at[:, span(peer * wide, wide)],
            wide_up.at[index],
            wide_ssem.at[peer],
            wide_rsem.at[index],
            peer,
        )

    def near_copy(peer, index):
        spot = lax.rem(peer, m)
        return remote(
            up.at[:, span(wide_total + spot * near, near)],
            near_up.at[index],
            near_ssem.at[spot],
            near_rsem.at[index],
            peer,
        )

    def sum_copy(other, index):
        return remote(
            sum_send.at[other],
            sum_recv.at[index],
            sum_ssem.at[other],
            sum_rsem.at[index],
            side * m + other // 2,
            lax.rem(other, 2),
        )

    def code_copy(peer, peer_core, code_side, code_seat):
        return remote(
            codes.at[side, seat],
            codes.at[code_side, code_seat],
            code_ssem.at[peer, peer_core],
            code_rsem.at[code_side, code_seat],
            peer,
            peer_core,
        )

    def back_copy(peer, index, which):
        kind, start, size = parts[which]
        send, recv = (near_send, near_recv) if kind else (wide_send, wide_recv)
        columns = pl.ds(start, size)
        return remote(
            send.at[peer, :, columns],
            recv.at[index, :, columns],
            back_ssem.at[peer, which],
            back_rsem.at[index, which],
            peer,
        )

    for peer in peers:
        tok_copy(peer, me).start()
    for peer in beside:
        down_copy(peer, place).start()

    def send_up(moment):
        for peer, when in zip(across, WIDE_ACROSS):
            if when == moment:
                wide_copy(peer, me).start()
        for peer, when in zip(beside, NEAR_BESIDE):
            if when == moment:
                near_copy(peer, place).start()
        for peer, when in zip(beside, WIDE_BESIDE):
            if when == moment:
                wide_copy(peer, me).start()

    send_up(0)

    loads[0].wait()
    for peer in beside:
        down_copy(peer, lax.rem(peer, m)).wait_recv()
    for peer in peers:
        tok_copy(peer, peer).wait_recv()
    send_up(1)
    arrived = tok_all[...]
    held = down_all[...].reshape(m * pair_rank, piece)
    product = lax.dot_general(
        arrived[:, :, :bit].reshape(total * 2, bit),
        jnp.concatenate([held[:, :bit], held[:, bit:]], axis=0),
        (((1,), (1,)), ((), ())),
        preferred_element_type=jnp.float32,
    ).reshape(n, 2, rows, 2 * LANES)
    slot_of = arrived[:, :, bit:].astype(jnp.float32).reshape(n, 2, rows, LANES)[:, 0]
    adapter = lax.broadcasted_iota(jnp.int32, (n, rows, LANES), 2) // pair_rank + side * m
    low = product[:, 0, :, :LANES] + product[:, 1, :, LANES:]
    low = jnp.where(slot_of == adapter.astype(jnp.float32), low, 0.0)
    sum_send[...] = low
    sum_recv[seat] = sum_send[seat]
    for other in seats:
        sum_copy(other, seat).start()
    send_up(2)
    for other in seats:
        sum_copy(other, other).wait_recv()
    codes[side, seat] = jnp.sum(sum_recv[...], axis=0)
    everyone = [(peer, peer_core) for peer in across for peer_core in (core, 1 - core)]
    everyone += [(peer, peer_core) for peer in beside for peer_core in (core, 1 - core)]
    everyone += [(me, 1 - core)]
    for peer, peer_core in everyone:
        code_copy(peer, peer_core, side, seat).start()
    send_up(3)

    def stacked(values):
        lane = lax.broadcasted_iota(jnp.int32, values.shape, 2)
        is_gate = lax.rem(lane, pair_rank) < pair_rank // 2
        both = [jnp.where(is_gate, values, 0.0), jnp.where(is_gate, 0.0, values)]
        return jnp.stack(both, axis=1).reshape(2 * total, values.shape[2]).astype(jnp.bfloat16)

    for other in seats:
        code_copy(side * m + other // 2, lax.rem(other, 2), side, other).wait_recv()
    near_codes = stacked(codes[side])
    loads[2].wait()
    for peer in beside:
        near_copy(peer, lax.rem(peer, m)).wait_recv()

    def expand(which, spread):
        kind, start, size = parts[which]
        source, send = (near_up, near_send) if kind else (wide_up, wide_send)
        columns = pl.ds(start, size)
        depth = spread.shape[1]
        delta = jnp.dot(
            spread,
            source[:, :, columns].reshape(depth, size),
            preferred_element_type=jnp.float32,
        )
        send[:, :, columns] = delta.astype(jnp.bfloat16).reshape(n, 2 * rows, size)
        for peer in across:
            back_copy(peer, me, which).start()
        if not LATE_BESIDE:
            for peer in beside:
                back_copy(peer, me, which).start()

    for which, (kind, _, _) in enumerate(parts):
        if kind:
            expand(which, near_codes)

    for other in range(n):
        code_copy((1 - side) * m + other // 2, other % 2, 1 - side, other).wait_recv()
    wide_codes = stacked(jnp.concatenate([codes[0], codes[1]], axis=2))
    loads[1].wait()
    for peer in peers:
        wide_copy(peer, peer).wait_recv()
    for which, (kind, _, _) in enumerate(parts):
        if not kind:
            expand(which, wide_codes)

    if LATE_BESIDE:
        for which in range(len(parts)):
            for peer in beside:
                back_copy(peer, me, which).start()
    loads[3].wait()
    loads[4].wait()

    def finish(start, size, block):
        columns = span(start, size)
        gate = gate_vmem[:, columns].astype(jnp.float32) + block[:rows]
        raised = up_vmem[:, columns].astype(jnp.float32) + block[rows:]
        out[:, columns] = (jax.nn.silu(gate) * raised).astype(out.dtype)

    for which, (kind, start, size) in enumerate(parts):
        columns = pl.ds(start, size)
        if kind:
            for step in range(m):
                spot = lax.rem(place + step, m)
                if step:
                    mine = side * m + spot
                    back_copy(mine, mine, which).wait_recv()
                    own = near_recv[mine, :, columns]
                else:
                    own = near_send[me, :, columns]
                far = (1 - side) * m + spot
                back_copy(far, far, which).wait_recv()
                block = own.astype(jnp.float32) + near_recv[far, :, columns].astype(jnp.float32)
                finish(wide_total + spot * near + start, size, block)
        else:
            own = wide_send[me, :, columns].astype(jnp.float32)
            finish(me * wide + start, size, own)
            for peer in beside + across:
                back_copy(peer, peer, which).wait_recv()
                block = wide_recv[peer, :, columns].astype(jnp.float32)
                finish(peer * wide + start, size, block)

    for peer in peers:
        tok_copy(peer, me).wait_send()
        wide_copy(peer, me).wait_send()
        for which in range(len(parts)):
            back_copy(peer, me, which).wait_send()
    for peer in beside:
        down_copy(peer, place).wait_send()
        near_copy(peer, place).wait_send()
    for other in seats:
        sum_copy(other, seat).wait_send()
    for peer, peer_core in everyone:
        code_copy(peer, peer_core, side, seat).wait_send()


def cut(size, pieces):
    tiles = size // LANES
    edges = [tiles * k // pieces * LANES for k in range(pieces + 1)]
    return [(a, b - a) for a, b in zip(edges, edges[1:]) if b > a]


WIDE_ACROSS = (0, 0, 2, 3)
NEAR_BESIDE = (0, 0, 2)
WIDE_BESIDE = (3, 3, 3)
LATE_BESIDE = 0
WIDE_TILES = 10
NEAR_PIECES = 1
WIDE_PIECES = 1


def local(mesh, *arrays):
    tokens, ids, storage, down, up, gate_base, up_base = arrays
    n = mesh.shape["dp"]
    rows, width = tokens.shape
    held, pair_rank, _ = down.shape
    hidden = up.shape[2]
    m = n // 2
    wide = WIDE_TILES * LANES
    near = (hidden - n * wide) // m
    fits = (
        held == 1
        and n % 2 == 0
        and n == rows == 8
        and mesh.shape["tensor"] == 2
        and m * pair_rank == LANES
        and width % (2 * m * LANES) == 0
        and near > 0
        and near % LANES == 0
        and n * wide + m * near == hidden
    )
    if not fits:
        return plain(*arrays)
    parts = [(1, *edge) for edge in cut(near, NEAR_PIECES)]
    parts += [(0, *edge) for edge in cut(wide, WIDE_PIECES)]
    count = len(parts)
    vmem = pl.BlockSpec(memory_space=pltpu.VMEM)
    hbm = pl.BlockSpec(memory_space=pl.ANY)
    dma = pltpu.SemaphoreType.DMA
    bf16 = jnp.bfloat16
    packed = width // (2 * m) + LANES
    return pl.pallas_call(
        functools.partial(kernel, n, parts),
        out_shape=jax.ShapeDtypeStruct((rows, hidden), bf16),
        in_specs=[hbm, hbm, hbm, hbm, hbm, hbm, hbm],
        out_specs=vmem,
        scratch_shapes=[
            pltpu.SMEM(ids.shape, ids.dtype),
            pltpu.SMEM(storage.shape, storage.dtype),
            pltpu.VMEM((rows, width), bf16),
            pltpu.VMEM((m, 2 * rows, packed), bf16),
            pltpu.VMEM((n, 2 * rows, packed), bf16),
            pltpu.VMEM((m, pair_rank, width // m), bf16),
            pltpu.VMEM((n, rows, LANES), jnp.float32),
            pltpu.VMEM((n, rows, LANES), jnp.float32),
            pltpu.VMEM((2, n, rows, LANES), jnp.float32),
            pltpu.VMEM((n, pair_rank, wide), bf16),
            pltpu.VMEM((m, pair_rank, near), bf16),
            pltpu.VMEM((n, 2 * rows, wide), bf16),
            pltpu.VMEM((n, 2 * rows, near), bf16),
            pltpu.VMEM((n, 2 * rows, wide), bf16),
            pltpu.VMEM((n, 2 * rows, near), bf16),
            pltpu.VMEM((rows, hidden), bf16),
            pltpu.VMEM((rows, hidden), bf16),
            dma((n,)),
            dma((n,)),
            dma((m,)),
            dma((m,)),
            dma((n,)),
            dma((n,)),
            dma((n, 2)),
            dma((2, n)),
            dma((n,)),
            dma((n,)),
            dma((m,)),
            dma((m,)),
            dma((n, count)),
            dma((n, count)),
            dma((8,)),
        ],
        compiler_params=pltpu.CompilerParams(
            collective_id=0, has_side_effects=True, vmem_limit_bytes=60 * 1024 * 1024
        ),
    )(ids, storage, tokens, down[0], up[0], gate_base, up_base)


def solution(mesh):
    in_specs = (
        P(("groups", "dp"), "tensor"),
        P(("groups", "dp")),
        P("groups"),
        P(("groups", "dp"), None, "tensor"),
        P(("groups", "dp"), None, "tensor"),
        P(("groups", "dp"), "tensor"),
        P(("groups", "dp"), "tensor"),
    )
    out_specs = P(("groups", "dp"), "tensor")
    return jax.shard_map(functools.partial(local, mesh), mesh=mesh, in_specs=in_specs, out_specs=out_specs, check_vma=False)
```

```python
import functools
import math

import jax
import jax.numpy as jnp
from jax import lax
from jax.experimental import pallas as pl
from jax.experimental.pallas import tpu as pltpu
from jax.sharding import PartitionSpec as P


def plain(
    tokens,
    request_adapter_index,
    adapter_storage_slot,
    adapter_down_weight,
    adapter_up_weight,
    gate_projected_base,
    up_projected_base,
):
    holding_count, paired_rank, half_rank_width = adapter_down_weight.shape
    rank_size = paired_rank // 2
    ids_all = lax.all_gather(request_adapter_index, "dp", axis=0, tiled=True)
    total_rows = ids_all.shape[0]
    adapter_count = adapter_storage_slot.shape[0]
    id_match = ids_all[:, None] == jnp.arange(adapter_count, dtype=jnp.int32)[None, :]
    slot_all = jnp.sum(jnp.where(id_match, adapter_storage_slot[None, :], 0), axis=1)
    flattened_down = adapter_down_weight.reshape(holding_count * paired_rank, half_rank_width)
    owner_index = lax.axis_index("dp")
    shard_rows = lax.all_gather(tokens, "dp", axis=0, tiled=True)
    row_count = shard_rows.shape[0]
    projected = jnp.einsum(
        "md,cd->mc", shard_rows, flattened_down, preferred_element_type=jnp.float32
    )
    projected = projected.reshape(row_count, holding_count, paired_rank)
    local_slot = slot_all - owner_index * holding_count
    picker = (local_slot[:, None] == jnp.arange(holding_count, dtype=jnp.int32)[None, :]).astype(
        jnp.float32
    )
    term_rows = jnp.sum(projected * picker[:, :, None], axis=1)
    low_rank = lax.psum(term_rows, ("dp", "tensor"))
    low_bf = low_rank.astype(jnp.bfloat16)
    up_cols = lax.all_to_all(
        adapter_up_weight.reshape(holding_count * paired_rank, adapter_up_weight.shape[2]),
        "dp",
        split_axis=1,
        concat_axis=0,
        tiled=True,
    )
    narrow = up_cols.shape[1]
    up_four = up_cols.reshape(adapter_count, 2, rank_size, narrow)
    block_row_span = math.gcd(total_rows, 256)
    block_count = total_rows // block_row_span
    adapter_range = jnp.arange(adapter_count, dtype=jnp.int32)

    def expand(block_args):
        low_block, storage_slot_block = block_args
        onehot = (storage_slot_block[:, None] == adapter_range[None, :]).astype(jnp.bfloat16)
        spread = onehot[:, :, None, None] * low_block.reshape(block_row_span, 1, 2, rank_size)
        update = jnp.einsum("rajk,ajkf->rjf", spread, up_four, preferred_element_type=jnp.float32)
        return update.astype(jnp.bfloat16)

    deltas = lax.map(
        expand,
        (
            low_bf.reshape(block_count, block_row_span, paired_rank),
            slot_all.reshape(block_count, block_row_span),
        ),
    )
    deltas = deltas.reshape(total_rows, 2, narrow)
    home_rows = lax.all_to_all(deltas, "dp", split_axis=0, concat_axis=2, tiled=True)
    gate_sum = gate_projected_base.astype(jnp.float32) + home_rows[:, 0].astype(jnp.float32)
    up_sum = up_projected_base.astype(jnp.float32) + home_rows[:, 1].astype(jnp.float32)
    return (jax.nn.silu(gate_sum) * up_sum).astype(jnp.bfloat16)


MESH = pl.DeviceIdType.MESH
LANES = 128


def kernel(
    n,
    parts,
    ids_hbm,
    storage_hbm,
    tokens,
    down,
    up,
    gate_base,
    up_base,
    out_hbm,
    out,
    out_sem,
    ids,
    storage,
    tok_vmem,
    tok_send,
    tok_all,
    down_all,
    sum_send,
    sum_recv,
    codes,
    wide_up,
    near_up,
    wide_send,
    near_send,
    wide_recv,
    near_recv,
    gate_vmem,
    up_vmem,
    tok_ssem,
    tok_rsem,
    down_ssem,
    down_rsem,
    sum_ssem,
    sum_rsem,
    code_ssem,
    code_rsem,
    wide_ssem,
    wide_rsem,
    near_ssem,
    near_rsem,
    back_ssem,
    back_rsem,
    local_sem,
):
    group = lax.axis_index("groups")
    me = lax.axis_index("dp")
    core = lax.axis_index("tensor")
    m = n // 2
    side, place = me // m, lax.rem(me, m)
    seat = place * 2 + core
    rows, width = tok_vmem.shape
    piece = width // m
    bit = piece // 2
    pair_rank = down.shape[0]
    wide, near = wide_up.shape[2], near_up.shape[2]
    wide_total = n * wide
    total = n * rows

    def remote(src, dst, send, recv, peer, peer_core=core):
        return pltpu.make_async_remote_copy(
            src_ref=src,
            dst_ref=dst,
            send_sem=send,
            recv_sem=recv,
            device_id=(group, peer, peer_core),
            device_id_type=MESH,
        )

    across = [(1 - side) * m + lax.rem(place + step, m) for step in range(m)]
    beside = [side * m + lax.rem(place + step, m) for step in range(1, m)]
    peers = across + beside
    seats = [lax.rem(seat + step, n) for step in range(1, n)]

    tok_load = pltpu.make_async_copy(tokens, tok_vmem, local_sem.at[0])
    tok_load.start()
    index_loads = [
        pltpu.make_async_copy(ids_hbm, ids, local_sem.at[6]),
        pltpu.make_async_copy(storage_hbm, storage, local_sem.at[7]),
    ]
    for copy in index_loads:
        copy.start()
    barrier = pltpu.get_barrier_semaphore()
    for peer in peers:
        for peer_core in range(2):
            pl.semaphore_signal(
                barrier, inc=1, device_id=(group, peer, peer_core), device_id_type=MESH
            )
    pl.semaphore_signal(barrier, inc=1, device_id=(group, me, 1 - core), device_id_type=MESH)

    def span(start, size):
        return pl.ds(pl.multiple_of(start, LANES), size)

    loads = [
        pltpu.make_async_copy(down.at[:, span(place * piece, piece)], down_all.at[place], local_sem.at[1]),
        pltpu.make_async_copy(up.at[:, span(me * wide, wide)], wide_up.at[me], local_sem.at[2]),
        pltpu.make_async_copy(
            up.at[:, span(wide_total + place * near, near)], near_up.at[place], local_sem.at[3]
        ),
        pltpu.make_async_copy(gate_base, gate_vmem, local_sem.at[4]),
        pltpu.make_async_copy(up_base, up_vmem, local_sem.at[5]),
    ]
    for copy in loads:
        copy.start()

    for copy in index_loads:
        copy.wait()
    slot_rows = lax.broadcasted_iota(jnp.int32, (rows, LANES), 0)
    slots = jnp.zeros((rows, LANES), jnp.int32)
    for row in range(rows):
        slots = jnp.where(slot_rows == row, storage[ids[row]], slots)
    slots = slots.astype(jnp.float32)
    tok_load.wait()
    values = tok_vmem[...].astype(jnp.float32)
    for part in range(m):
        cut_at = part * piece
        tok_send[part] = jnp.concatenate(
            [
                jnp.concatenate([values[:, cut_at : cut_at + bit], slots], axis=1),
                jnp.concatenate([values[:, cut_at + bit : cut_at + piece], slots], axis=1),
            ],
            axis=0,
        ).astype(jnp.bfloat16)
    tok_all[me] = tok_send[place]

    pl.semaphore_wait(barrier, 2 * n - 1)

    def tok_copy(peer, index):
        return remote(
            tok_send.at[lax.rem(peer, m)], tok_all.at[index], tok_ssem.at[peer], tok_rsem.at[index], peer
        )

    def down_copy(peer, index):
        spot = lax.rem(peer, m)
        return remote(
            down.at[:, span(spot * piece, piece)],
            down_all.at[index],
            down_ssem.at[spot],
            down_rsem.at[index],
            peer,
        )

    def wide_copy(peer, index):
        return remote(
            up.at[:, span(peer * wide, wide)],
            wide_up.at[index],
            wide_ssem.at[peer],
            wide_rsem.at[index],
            peer,
        )

    def near_copy(peer, index):
        spot = lax.rem(peer, m)
        return remote(
            up.at[:, span(wide_total + spot * near, near)],
            near_up.at[index],
            near_ssem.at[spot],
            near_rsem.at[index],
            peer,
        )

    def sum_copy(other, index):
        return remote(
            sum_send.at[other],
            sum_recv.at[index],
            sum_ssem.at[other],
            sum_rsem.at[index],
            side * m + other // 2,
            lax.rem(other, 2),
        )

    def code_copy(peer, peer_core, code_side, code_seat):
        return remote(
            codes.at[side, seat],
            codes.at[code_side, code_seat],
            code_ssem.at[peer, peer_core],
            code_rsem.at[code_side, code_seat],
            peer,
            peer_core,
        )

    def back_copy(peer, index, which):
        kind, start, size = parts[which]
        send, recv = (near_send, near_recv) if kind else (wide_send, wide_recv)
        columns = pl.ds(start, size)
        return remote(
            send.at[peer, :, columns],
            recv.at[index, :, columns],
            back_ssem.at[peer, which],
            back_rsem.at[index, which],
            peer,
        )

    for peer in peers:
        tok_copy(peer, me).start()
    for peer in beside:
        down_copy(peer, place).start()

    def send_up(moment):
        for peer, when in zip(across, WIDE_ACROSS):
            if when == moment:
                wide_copy(peer, me).start()
        for peer, when in zip(beside, NEAR_BESIDE):
            if when == moment:
                near_copy(peer, place).start()
        for peer, when in zip(beside, WIDE_BESIDE):
            if when == moment:
                wide_copy(peer, me).start()

    send_up(0)

    loads[0].wait()
    for peer in beside:
        down_copy(peer, lax.rem(peer, m)).wait_recv()
    for peer in peers:
        tok_copy(peer, peer).wait_recv()
    send_up(1)
    arrived = tok_all[...]
    held = down_all[...].reshape(m * pair_rank, piece)
    product = lax.dot_general(
        arrived[:, :, :bit].reshape(total * 2, bit),
        jnp.concatenate([held[:, :bit], held[:, bit:]], axis=0),
        (((1,), (1,)), ((), ())),
        preferred_element_type=jnp.float32,
    ).reshape(n, 2, rows, 2 * LANES)
    slot_of = arrived[:, :, bit:].astype(jnp.float32).reshape(n, 2, rows, LANES)[:, 0]
    adapter = lax.broadcasted_iota(jnp.int32, (n, rows, LANES), 2) // pair_rank + side * m
    low = product[:, 0, :, :LANES] + product[:, 1, :, LANES:]
    low = jnp.where(slot_of == adapter.astype(jnp.float32), low, 0.0)
    sum_send[...] = low
    sum_recv[seat] = sum_send[seat]
    for other in seats:
        sum_copy(other, seat).start()
    send_up(2)
    for other in seats:
        sum_copy(other, other).wait_recv()
    codes[side, seat] = jnp.sum(sum_recv[...], axis=0)
    everyone = [(peer, peer_core) for peer in across for peer_core in (core, 1 - core)]
    everyone += [(peer, peer_core) for peer in beside for peer_core in (core, 1 - core)]
    everyone += [(me, 1 - core)]
    for peer, peer_core in everyone:
        code_copy(peer, peer_core, side, seat).start()
    send_up(3)

    def stacked(values):
        lane = lax.broadcasted_iota(jnp.int32, values.shape, 2)
        is_gate = lax.rem(lane, pair_rank) < pair_rank // 2
        both = [jnp.where(is_gate, values, 0.0), jnp.where(is_gate, 0.0, values)]
        return jnp.stack(both, axis=1).reshape(2 * total, values.shape[2]).astype(jnp.bfloat16)

    for other in seats:
        code_copy(side * m + other // 2, lax.rem(other, 2), side, other).wait_recv()
    near_codes = stacked(codes[side])
    loads[2].wait()
    for peer in beside:
        near_copy(peer, lax.rem(peer, m)).wait_recv()

    def expand(which, spread):
        kind, start, size = parts[which]
        source, send = (near_up, near_send) if kind else (wide_up, wide_send)
        columns = pl.ds(start, size)
        depth = spread.shape[1]
        delta = jnp.dot(
            spread,
            source[:, :, columns].reshape(depth, size),
            preferred_element_type=jnp.float32,
        )
        send[:, :, columns] = delta.astype(jnp.bfloat16).reshape(n, 2 * rows, size)
        for peer in across:
            back_copy(peer, me, which).start()
        if not LATE_BESIDE:
            for peer in beside:
                back_copy(peer, me, which).start()

    for which, (kind, _, _) in enumerate(parts):
        if kind:
            expand(which, near_codes)

    for other in range(n):
        code_copy((1 - side) * m + other // 2, other % 2, 1 - side, other).wait_recv()
    wide_codes = stacked(jnp.concatenate([codes[0], codes[1]], axis=2))
    loads[1].wait()
    for peer in peers:
        wide_copy(peer, peer).wait_recv()
    for which, (kind, _, _) in enumerate(parts):
        if not kind:
            expand(which, wide_codes)

    if LATE_BESIDE:
        for which in range(len(parts)):
            for peer in beside:
                back_copy(peer, me, which).start()
    loads[3].wait()
    loads[4].wait()

    stores = []

    def finish(start, size, block):
        columns = span(start, size)
        gate = gate_vmem[:, columns].astype(jnp.float32) + block[:rows]
        raised = up_vmem[:, columns].astype(jnp.float32) + block[rows:]
        out[:, columns] = (jax.nn.silu(gate) * raised).astype(out.dtype)
        stores.append(
            pltpu.make_async_copy(
                out.at[:, columns], out_hbm.at[:, columns], out_sem.at[len(stores)]
            )
        )
        stores[-1].start()

    for which, (kind, start, size) in enumerate(parts):
        columns = pl.ds(start, size)
        if kind:
            for step in range(m):
                spot = lax.rem(place + step, m)
                if step:
                    mine = side * m + spot
                    back_copy(mine, mine, which).wait_recv()
                    own = near_recv[mine, :, columns]
                else:
                    own = near_send[me, :, columns]
                far = (1 - side) * m + spot
                back_copy(far, far, which).wait_recv()
                block = own.astype(jnp.float32) + near_recv[far, :, columns].astype(jnp.float32)
                finish(wide_total + spot * near + start, size, block)
        else:
            own = wide_send[me, :, columns].astype(jnp.float32)
            finish(me * wide + start, size, own)
            for peer in beside + across:
                back_copy(peer, peer, which).wait_recv()
                block = wide_recv[peer, :, columns].astype(jnp.float32)
                finish(peer * wide + start, size, block)

    for copy in stores:
        copy.wait()
    for peer in peers:
        tok_copy(peer, me).wait_send()
        wide_copy(peer, me).wait_send()
        for which in range(len(parts)):
            back_copy(peer, me, which).wait_send()
    for peer in beside:
        down_copy(peer, place).wait_send()
        near_copy(peer, place).wait_send()
    for other in seats:
        sum_copy(other, seat).wait_send()
    for peer, peer_core in everyone:
        code_copy(peer, peer_core, side, seat).wait_send()


def cut(size, pieces):
    tiles = size // LANES
    edges = [tiles * k // pieces * LANES for k in range(pieces + 1)]
    return [(a, b - a) for a, b in zip(edges, edges[1:]) if b > a]


WIDE_ACROSS = (0, 0, 2, 3)
NEAR_BESIDE = (0, 0, 2)
WIDE_BESIDE = (3, 3, 3)
LATE_BESIDE = 0
WIDE_TILES = 10
NEAR_PIECES = 1
WIDE_PIECES = 1


def local(mesh, *arrays):
    tokens, ids, storage, down, up, gate_base, up_base = arrays
    n = mesh.shape["dp"]
    rows, width = tokens.shape
    held, pair_rank, _ = down.shape
    hidden = up.shape[2]
    m = n // 2
    wide = WIDE_TILES * LANES
    near = (hidden - n * wide) // m
    fits = (
        held == 1
        and n % 2 == 0
        and n == rows == 8
        and mesh.shape["tensor"] == 2
        and m * pair_rank == LANES
        and width % (2 * m * LANES) == 0
        and near > 0
        and near % LANES == 0
        and n * wide + m * near == hidden
    )
    if not fits:
        return plain(*arrays)
    parts = [(1, *edge) for edge in cut(near, NEAR_PIECES)]
    parts += [(0, *edge) for edge in cut(wide, WIDE_PIECES)]
    count = len(parts)
    hbm = pl.BlockSpec(memory_space=pl.ANY)
    dma = pltpu.SemaphoreType.DMA
    bf16 = jnp.bfloat16
    packed = width // (2 * m) + LANES
    return pl.pallas_call(
        functools.partial(kernel, n, parts),
        out_shape=jax.ShapeDtypeStruct((rows, hidden), bf16),
        in_specs=[hbm, hbm, hbm, hbm, hbm, hbm, hbm],
        out_specs=hbm,
        scratch_shapes=[
            pltpu.VMEM((rows, hidden), bf16),
            dma((count * n,)),
            pltpu.SMEM(ids.shape, ids.dtype),
            pltpu.SMEM(storage.shape, storage.dtype),
            pltpu.VMEM((rows, width), bf16),
            pltpu.VMEM((m, 2 * rows, packed), bf16),
            pltpu.VMEM((n, 2 * rows, packed), bf16),
            pltpu.VMEM((m, pair_rank, width // m), bf16),
            pltpu.VMEM((n, rows, LANES), jnp.float32),
            pltpu.VMEM((n, rows, LANES), jnp.float32),
            pltpu.VMEM((2, n, rows, LANES), jnp.float32),
            pltpu.VMEM((n, pair_rank, wide), bf16),
            pltpu.VMEM((m, pair_rank, near), bf16),
            pltpu.VMEM((n, 2 * rows, wide), bf16),
            pltpu.VMEM((n, 2 * rows, near), bf16),
            pltpu.VMEM((n, 2 * rows, wide), bf16),
            pltpu.VMEM((n, 2 * rows, near), bf16),
            pltpu.VMEM((rows, hidden), bf16),
            pltpu.VMEM((rows, hidden), bf16),
            dma((n,)),
            dma((n,)),
            dma((m,)),
            dma((m,)),
            dma((n,)),
            dma((n,)),
            dma((n, 2)),
            dma((2, n)),
            dma((n,)),
            dma((n,)),
            dma((m,)),
            dma((m,)),
            dma((n, count)),
            dma((n, count)),
            dma((8,)),
        ],
        compiler_params=pltpu.CompilerParams(
            collective_id=0, has_side_effects=True, vmem_limit_bytes=60 * 1024 * 1024
        ),
    )(ids, storage, tokens, down[0], up[0], gate_base, up_base)


def solution(mesh):
    in_specs = (
        P(("groups", "dp"), "tensor"),
        P(("groups", "dp")),
        P("groups"),
        P(("groups", "dp"), None, "tensor"),
        P(("groups", "dp"), None, "tensor"),
        P(("groups", "dp"), "tensor"),
        P(("groups", "dp"), "tensor"),
    )
    out_specs = P(("groups", "dp"), "tensor")
    return jax.shard_map(functools.partial(local, mesh), mesh=mesh, in_specs=in_specs, out_specs=out_specs, check_vma=False)
```
